128 devices in a mesh: section: 4 (over x_lo, core), seq: 32 (over z, y, x_hi).
Axes of the slice: x: 4 (x_hi: 2, x_lo: 2; x = x_hi * 2 + x_lo), y: 4, z: 4, core: 2. Of those that a mesh axis runs over, the one named last changes fastest.
Arguments:
- saved_q: bfloat16 [4, 2, 2, 4096, 2048], P('section', None, None, 'seq'), may hold values from -6 to 6
- saved_k: bfloat16 [4, 2, 2, 4096, 2048], P('section', None, None, 'seq'), may hold values from -6 to 6
- saved_v: bfloat16 [4, 2, 2, 4096, 2048], P('section', None, None, 'seq'), may hold values from -6 to 6
- saved_o: bfloat16 [4, 2, 2, 4096, 2048], P('section', None, None, 'seq'), may hold values from -1.796875 to 1.796875
- saved_lse: float32 [4, 2, 2, 4096, 16], P('section', None, None, 'seq'), as said below
- cotangent: bfloat16 [4, 2, 4096, 3072], P('section', None, 'seq'), may hold values from -24 to 24
- out_weight: bfloat16 [4, 2048, 3072], P('section', 'seq'), may hold values from -0.125 to 0.125
- plan: int32 [4], P('section'), may hold values from 0 to 1
- control_map: int32 [5], replicated, may hold values from 0 to 3
- control_scale: float32 [5], replicated, may hold values from 0.25 to 1
Outputs:
- grad_q: bfloat16 [4, 2, 4096, 2048], P('section', None, 'seq')
- grad_k: bfloat16 [4, 2, 4096, 2048], P('section', None, 'seq')
- grad_v: bfloat16 [4, 2, 4096, 2048], P('section', None, 'seq')
- control_grad: bfloat16 [5, 2, 4096, 3072], P(None, None, 'seq', 'section')
The draws below stay inside these ranges and needn't reach their ends.
Inputs may be any that keep to these rules, and one draw needn't show every extreme that they name: `saved_lse`: each value lies between the natural logarithm of 4096 and that plus one.
All inputs are finite; a program needn't handle non-finite values.
Results may differ from the reference program's by a relative error of at most 0.0061.
Values may be sent and summed in bfloat16 or wider, within the bound.
A program may use at most 128 MiB of HBM per device.

```python
import math
import jax
import jax.numpy as jnp
from jax import lax

D = 3072
HEADS = 16
HD = 128
W = 2048
IMAGES = 2
TOKENS = 4096
SECTIONS = 4
MB = 2
NCTRL = 5


def draw_saved_lse(key, part):
    key = jax.random.fold_in(key, 11)
    offset = jnp.log(jnp.float32(TOKENS))
    jitter = jax.random.uniform(key, (SECTIONS, MB, IMAGES, TOKENS, HEADS), jnp.float32, 0.25, 0.75)
    return offset + jitter


def place_ends(result, stream_key, smallest, top_value):
    extent = result.shape
    place = [jax.random.randint(jax.random.fold_in(stream_key, axis), (), 0, extent[axis]) for axis in range(len(extent))]
    result = result.at[tuple(place)].set(smallest)
    longest = extent.index(max(extent))
    place[longest] = (place[longest] + 1) % extent[longest]
    return result.at[tuple(place)].set(top_value)


def shard_levels(rng, dims, cuts, smallest, high):
    level, own = 1.0, jax.random.fold_in(rng, 6)
    for axis_at, blocks in cuts:
        draws = jnp.exp(jax.random.uniform(jax.random.fold_in(own, axis_at), (blocks,), jnp.float32, smallest / len(cuts), high / len(cuts)))
        level = level * jnp.repeat(draws, dims[axis_at] // blocks).reshape([-1 if axis == axis_at else 1 for axis in range(len(dims))])
    return level


def centred(stream_key, shape, scale, bound, shards=(), held_as=jnp.bfloat16):
    entries = jax.random.normal(stream_key, shape, jnp.float32) * scale
    if len(shards) > 0:
        entries = shard_levels(stream_key, shape, shards, -0.22, 0.18) * entries
    return jnp.clip(entries, min=-bound, max=bound).astype(held_as)


def setup_inputs(seed: int = 0) -> dict:
    streams_of = jax.random.split(jax.random.key(seed), 11)
    saved_q = centred(streams_of[0], (SECTIONS, MB, IMAGES, TOKENS, W), 1.0, 6.0, ((0, 4), (3, 32)))
    saved_k = centred(streams_of[1], (SECTIONS, MB, IMAGES, TOKENS, W), 1.0, 6.0, ((0, 4), (3, 32)))
    saved_v = centred(streams_of[2], (SECTIONS, MB, IMAGES, TOKENS, W), 1.0, 6.0, ((0, 4), (3, 32)))
    saved_o = centred(streams_of[3], (SECTIONS, MB, IMAGES, TOKENS, W), 0.3, 1.796875, ((0, 4), (3, 32)))
    saved_lse = draw_saved_lse(jax.random.fold_in(streams_of[10], 71), 0)
    cotangent = centred(streams_of[5], (SECTIONS, IMAGES, TOKENS, D), 4.0, 24.0, ((0, 4), (2, 32)))
    out_weight = centred(streams_of[6], (SECTIONS, W, D), W ** -0.5, 0.125, ((0, 4), (1, 32)))
    plan = place_ends(jax.random.randint(streams_of[7], (SECTIONS,), 0, MB), jax.random.fold_in(streams_of[7], 1), 0, MB - 1).astype(jnp.int32)
    control_map = place_ends(jax.random.randint(streams_of[8], (NCTRL,), 0, SECTIONS), jax.random.fold_in(streams_of[8], 1), 0, SECTIONS - 1).astype(jnp.int32)
    control_scale = jnp.clip(jnp.exp(jax.random.uniform(streams_of[9], (NCTRL,), jnp.float32, math.log(0.25), math.log(1.0))), 0.25, 1.0)
    return dict(saved_q=saved_q, saved_k=saved_k, saved_v=saved_v, saved_o=saved_o, saved_lse=saved_lse, cotangent=cotangent, out_weight=out_weight, plan=plan, control_map=control_map, control_scale=control_scale)


def split_heads(array):
    return array.reshape(TOKENS, HEADS, HD).transpose(1, 0, 2)


def join_heads(array):
    return array.transpose(1, 0, 2).reshape(TOKENS, W)


def head_grads(query, keys, values, grads, lse, delta):
    scale = HD ** -0.5
    block_rows = min(512, TOKENS)
    count = TOKENS // block_rows
    blocks = (query.reshape(count, block_rows, HD), grads.reshape(count, block_rows, HD),
              lse.reshape(count, block_rows), delta.reshape(count, block_rows))

    def block_step(carry, block):
        query_block, grads_block, lse_block, delta_block = block
        scores = jnp.dot(query_block, keys.T, preferred_element_type=jnp.float32) * scale
        probs = jnp.exp(scores - lse_block[:, None])
        grad_value = jnp.dot(probs.astype(jnp.bfloat16).T, grads_block, preferred_element_type=jnp.float32)
        grad_probs = jnp.dot(grads_block, values.T, preferred_element_type=jnp.float32)
        grad_scores = (probs * (grad_probs - delta_block[:, None])).astype(jnp.bfloat16)
        grad_key = jnp.dot(grad_scores.T, query_block, preferred_element_type=jnp.float32) * scale
        grad_query = (jnp.dot(grad_scores, keys, preferred_element_type=jnp.float32) * scale).astype(jnp.bfloat16)
        return (carry[0] + grad_key, carry[1] + grad_value), grad_query

    zeros_sum = jnp.zeros((TOKENS, HD), jnp.float32)
    (key_sum, value_sum), query_parts = lax.scan(block_step, (zeros_sum, zeros_sum), blocks)
    return query_parts.reshape(TOKENS, HD), key_sum.astype(jnp.bfloat16), value_sum.astype(jnp.bfloat16)


def reference(saved_q, saved_k, saved_v, saved_o, saved_lse, cotangent, out_weight, plan, control_map, control_scale):
    section_query, section_key, section_value = [], [], []
    for section_index in range(SECTIONS):
        picked = plan[section_index]
        flat_out = cotangent[section_index].reshape(IMAGES * TOKENS, D)
        grad_attn = jnp.dot(flat_out, out_weight[section_index].T, preferred_element_type=jnp.float32)
        grad_attn = grad_attn.astype(jnp.bfloat16).reshape(IMAGES, TOKENS, W)
        image_query, image_key, image_value = [], [], []
        for image_index in range(IMAGES):
            query = saved_q[section_index, picked, image_index]
            keys = saved_k[section_index, picked, image_index]
            values = saved_v[section_index, picked, image_index]
            output = saved_o[section_index, picked, image_index]
            grads = grad_attn[image_index]
            delta = jnp.sum((grads.astype(jnp.float32) * output.astype(jnp.float32)).reshape(TOKENS, HEADS, HD), axis=2).T
            lse = saved_lse[section_index, picked, image_index].T
            parts = lax.map(lambda items: head_grads(*items),
                            (split_heads(query), split_heads(keys), split_heads(values), split_heads(grads), lse, delta))
            image_query.append(join_heads(parts[0]))
            image_key.append(join_heads(parts[1]))
            image_value.append(join_heads(parts[2]))
        section_query.append(jnp.stack(image_query))
        section_key.append(jnp.stack(image_key))
        section_value.append(jnp.stack(image_value))
    matched = cotangent[control_map].astype(jnp.float32)
    control_grad = (control_scale[:, None, None, None] * matched).astype(jnp.bfloat16)
    return jnp.stack(section_query), jnp.stack(section_key), jnp.stack(section_value), control_grad
```

```python
import functools
import math

import jax
import jax.numpy as jnp
from jax import lax
from jax.experimental import pallas as pl
from jax.experimental.pallas import tpu as pltpu
from jax.sharding import PartitionSpec as P

F32 = jnp.float32
BF16 = jnp.bfloat16
NT = (((1,), (1,)), ((), ()))
NN = (((1,), (0,)), ((), ()))


def dot(a, b, dims):
    return lax.dot_general(a, b, dims, preferred_element_type=F32)


def attention_kernel(block_keys, block_queries, unroll, q, k, v, g, stats, dq, dk, dv, dq_sum):
    total, head_size = q.shape
    scale = head_size**-0.5
    scale2 = scale * math.log2(math.e)
    dq_sum[...] = jnp.zeros_like(dq_sum)

    @pl.loop(0, total // block_keys)
    def _(u):
        us = pl.ds(pl.multiple_of(u * block_keys, block_keys), block_keys)
        kb, vb = k[us, :], v[us, :]
        kt = kb.T

        def inner(t, carry):
            sum_k, sum_v = carry
            ts = pl.ds(pl.multiple_of(t * block_queries, block_queries), block_queries)
            qb, gb = q[ts, :], g[ts, :]
            p = jnp.exp2(dot(kb, qb, NT) * scale2 - stats[0:1, ts])
            sum_v = sum_v + dot(p.astype(BF16), gb, NN)
            ds = (p * (dot(vb, gb, NT) - stats[1:2, ts])).astype(BF16)
            sum_k = sum_k + dot(ds, qb, NN)
            dq_sum[:, ts] += dot(kt, ds, NN)
            return sum_k, sum_v

        zeros = jnp.zeros((block_keys, head_size), F32)
        sum_k, sum_v = lax.fori_loop(0, total // block_queries, inner, (zeros, zeros), unroll=unroll)
        dk[us, :] = (sum_k * scale).astype(BF16)
        dv[us, :] = sum_v.astype(BF16)

    dq[...] = (dq_sum[...] * scale).astype(BF16).T


def attention_grads(q, k, v, g, stats):
    total, head_size = q.shape
    out = jax.ShapeDtypeStruct((total, head_size), BF16)
    whole = pl.BlockSpec(memory_space=pltpu.VMEM)
    return pl.pallas_call(
        functools.partial(attention_kernel, 1024, 512, 4),
        out_shape=(out, out, out),
        in_specs=[whole] * 5,
        out_specs=(whole, whole, whole),
        scratch_shapes=[pltpu.VMEM((head_size, total), F32)],
        compiler_params=pltpu.CompilerParams(vmem_limit_bytes=56 * 2**20),
        cost_estimate=pl.CostEstimate(
            flops=10 * total * total * head_size, bytes_accessed=16 * total * head_size, transcendentals=0
        ),
        name="attention_grads",
    )(q, k, v, g, stats)


def to_heads(array, head_count):
    images, rows, width = array.shape
    head_size = width // head_count
    shaped = array.reshape(images, rows, head_count, head_size).transpose(0, 2, 1, 3)
    return shaped.reshape(images * head_count, rows, head_size)


def to_tokens(array, images):
    count, rows, head_size = array.shape
    head_count = count // images
    shaped = array.reshape(images, head_count, rows, head_size).transpose(0, 2, 1, 3)
    return shaped.reshape(images, rows, head_count * head_size)


def shards(
    saved_q,
    saved_k,
    saved_v,
    saved_o,
    saved_lse,
    cotangent,
    out_weight,
    plan,
    control_map,
    control_scale,
):
    picked = plan[0]

    def select(array):
        return lax.dynamic_index_in_dim(array[0], picked, 0, keepdims=False)

    def exchange(array):
        return lax.all_to_all(array, "seq", split_axis=0, concat_axis=0, tiled=True)

    lse_rows = select(saved_lse)
    output_rows = select(saved_o)
    grad_out = cotangent[0]
    images, local_rows, depth = grad_out.shape
    head_count = lse_rows.shape[2]
    width = output_rows.shape[2]
    head_size = width // head_count
    weight = lax.all_gather(out_weight[0], "seq", axis=0, tiled=True)
    grad_attn = dot(grad_out.reshape(images * local_rows, depth), weight, NT)
    grad_attn = grad_attn.astype(BF16).reshape(images, local_rows, width)
    products = grad_attn.astype(F32) * output_rows.astype(F32)
    delta = jnp.sum(products.reshape(images, local_rows, head_count, head_size), axis=3)
    stats = jnp.stack([lse_rows * math.log2(math.e), delta], axis=3)
    stats = stats.transpose(0, 2, 3, 1).reshape(images * head_count, 2, local_rows)
    q, k, v, g = (
        exchange(to_heads(rows, head_count)).reshape(-1, head_size)
        for rows in (select(saved_q), select(saved_k), select(saved_v), grad_attn)
    )
    stats = exchange(stats).transpose(1, 0, 2).reshape(2, -1)
    grads = attention_grads(q, k, v, g, stats)
    backs = tuple(
        to_tokens(exchange(grad.reshape(-1, local_rows, head_size)), images)[None] for grad in grads
    )
    sections = lax.axis_size("section")
    pieces = grad_out.reshape(images, local_rows, sections, depth // sections).transpose(2, 0, 1, 3)
    pieces = lax.all_to_all(pieces, "section", split_axis=0, concat_axis=0, tiled=True)
    matched = jnp.take(pieces, control_map, axis=0, mode="clip").astype(F32)
    control_grad = (control_scale[:, None, None, None] * matched).astype(BF16)
    return (*backs, control_grad)


def solution(mesh):
    placed = (
        P("section", None, None, "seq", None),
        P("section", None, None, "seq", None),
        P("section", None, None, "seq", None),
        P("section", None, None, "seq", None),
        P("section", None, None, "seq", None),
        P("section", None, "seq", None),
        P("section", "seq", None),
        P("section"),
        P(),
        P(),
    )
    return jax.shard_map(
        shards,
        mesh=mesh,
        in_specs=placed,
        out_specs=(
            P("section", None, "seq", None),
            P("section", None, "seq", None),
            P("section", None, "seq", None),
            P(None, None, "seq", "section"),
        ),
        check_vma=False,
    )
```

```python
import functools
import math

import jax
import jax.numpy as jnp
from jax import lax
from jax.experimental import pallas as pl
from jax.experimental.pallas import tpu as pltpu
from jax.sharding import PartitionSpec as P

F32 = jnp.float32
BF16 = jnp.bfloat16
NT = (((1,), (1,)), ((), ()))
NN = (((1,), (0,)), ((), ()))


def dot(a, b, dims):
    return lax.dot_general(a, b, dims, preferred_element_type=F32)


def ring_offset(i):
    return i + (i // 2) * (1 - 2 * (i % 2))


def kernel(
    plan,
    control_map,
    control_scale,
    q_in,
    k_in,
    v_in,
    o_in,
    lse_in,
    cot_in,
    w_in,
    dq_out,
    dk_out,
    dv_out,
    control_out,
    q_two,
    k_two,
    v_two,
    o_two,
    lse_two,
    cot,
    w,
    q_send,
    k_send,
    v_send,
    g_send,
    stat_send,
    q,
    k,
    v,
    g,
    stat,
    lse_row,
    delta_row,
    dq_sum,
    pieces,
    load_sem,
    swap_s,
    swap_r,
    ring_s,
    ring_r,
    heads_s,
    heads_r,
    back_s,
    back_r,
    own_sem,
    piece_s,
    piece_r,
):
    me = lax.axis_index("seq")
    section = lax.axis_index("section")
    z, y, x = me // 8, (me // 2) % 4, me % 2
    devices, rows, head_size = q.shape
    heads = devices // 2
    half_rows = rows // 2
    half_depth = w.shape[4]
    scale = head_size**-0.5
    scale2 = scale * math.log2(math.e)

    def index_of(z, y, x):
        return ((z + 4) % 4) * 8 + ((y + 4) % 4) * 2 + x % 2

    def peer(step):
        return index_of(z + step // 8, y + (step // 2) % 4, x + step % 2)

    def columns(head):
        return pl.ds(pl.multiple_of(head * head_size, head_size), head_size)

    def remote(src, dst, send, recv, device):
        return pltpu.make_async_remote_copy(
            src_ref=src,
            dst_ref=dst,
            send_sem=send,
            recv_sem=recv,
            device_id=device,
            device_id_type=pl.DeviceIdType.MESH,
        )

    def local(src, dst, sem):
        return pltpu.make_async_copy(src, dst, sem)

    loads = [
        local(src, dst, load_sem.at[i])
        for i, (src, dst) in enumerate(
            ((k_in, k_two), (q_in, q_two), (v_in, v_two), (o_in, o_two), (lse_in, lse_two), (cot_in, cot))
        )
    ]
    for load in loads:
        load.start()
    my_rows = pl.ds(pl.multiple_of(x * half_rows, half_rows), half_rows)
    other_rows = pl.ds(pl.multiple_of((1 - x) * half_rows, half_rows), half_rows)

    def part_columns(part):
        return pl.ds(part * half_depth, half_depth)

    own_w = [local(w_in.at[:, part_columns(p)], w.at[p, z, y, my_rows], load_sem.at[6 + p]) for p in range(2)]
    for copy in own_w:
        copy.start()
    barrier = pltpu.get_barrier_semaphore()

    @pl.loop(1, devices)
    def _(step):
        pl.semaphore_signal(
            barrier, inc=1, device_id={"seq": peer(step)}, device_id_type=pl.DeviceIdType.MESH
        )

    @pl.loop(1, 4)
    def _(step):
        pl.semaphore_signal(
            barrier, inc=1, device_id={"section": (section + step) % 4}, device_id_type=pl.DeviceIdType.MESH
        )

    pl.semaphore_wait(barrier, devices + 2)

    swaps = [
        remote(
            w_in.at[:, part_columns(p)], w.at[p, z, y, my_rows], swap_s.at[p], swap_r.at[p], {"seq": index_of(z, y, x + 1)}
        )
        for p in range(2)
    ]
    for copy in swaps:
        copy.start()

    def turn(part, first, second):
        return (first, second) if part == 0 else (second, first)

    def block(part, first, second):
        dz, dy = turn(part, first, second)
        return w.at[part, (z + dz + 4) % 4, (y + dy + 4) % 4]

    def hop(part, where, to, rows_of, sem, src=None):
        dst = block(part, *where)
        if rows_of is not None:
            dst = dst.at[rows_of]
        dz, dy = turn(part, *to)
        return remote(
            dst if src is None else src,
            dst,
            ring_s.at[part, sem],
            ring_r.at[part, sem],
            {"seq": index_of(z + dz, y + dy, x)},
        )

    low, high = pl.ds(0, half_rows), pl.ds(half_rows, half_rows)
    first, second, forward = {}, {}, {}
    for p in range(2):
        src = w_in.at[:, part_columns(p)]
        first[p] = [hop(p, (0, 0), (1, 0), my_rows, 0, src), hop(p, (0, 0), (-1, 0), my_rows, 1, src)]
        for copy in first[p]:
            copy.start()

    def select(two, send, held, sem):
        picked = plan[0]

        @pl.loop(0, 2)
        def _(image):
            for head in range(heads):
                send[image * heads + head] = two[picked, image, :, head * head_size : (head + 1) * head_size]

        held[me] = send[me]

        @pl.loop(1, devices)
        def _(step):
            to = peer(step)
            remote(send.at[to], held.at[me], heads_s.at[sem], heads_r.at[sem], {"seq": to}).start()

    def arrived(send, held, sem):
        some = pl.ds(0, devices - 1)
        local(held.at[some], held.at[some], heads_r.at[sem]).wait()
        local(send.at[some], send.at[some], heads_s.at[sem]).wait()

    loads[0].wait()
    select(k_two, k_send, k, 0)
    loads[1].wait()
    select(q_two, q_send, q, 1)

    def start_second(p, group):
        at = ring_offset(group)
        second[p, group] = [
            hop(p, (at, 0), (0, 1), None, 6 + 4 * group),
            hop(p, (at, 0), (0, -1), None, 7 + 4 * group),
        ]
        for copy in second[p, group]:
            copy.start()

    for copy in own_w:
        copy.wait()
    for p in range(2):
        swaps[p].wait_recv()
        first[p] += [hop(p, (0, 0), (1, 0), other_rows, 2), hop(p, (0, 0), (-1, 0), other_rows, 3)]
        for copy in first[p][2:]:
            copy.start()
        start_second(p, 0)
    loads[2].wait()
    select(v_two, v_send, v, 2)
    for load in loads[3:]:
        load.wait()
    for p in range(2):
        first[p][0].wait_recv()
        first[p][2].wait_recv()
        first[p].append(hop(p, (-1, 0), (1, 0), low, 4))
        first[p][4].start()
        first[p][1].wait_recv()
        first[p][3].wait_recv()
        first[p].append(hop(p, (1, 0), (-1, 0), high, 5))
        first[p][5].start()
    for p in range(2):
        start_second(p, 1)
        start_second(p, 2)

    def start_forward(group):
        at = ring_offset(group)
        for p in range(2):
            second[p, group][0].wait_recv()
            forward[p, group] = [hop(p, (at, -1), (0, 1), low, 8 + 4 * group)]
            forward[p, group][0].start()
            second[p, group][1].wait_recv()
            forward[p, group].append(hop(p, (at, 1), (0, -1), high, 9 + 4 * group))
            forward[p, group][1].start()

    def project(dz, dy):
        zz, yy = (z + dz + 4) % 4, (y + dy + 4) % 4
        head = zz * 4 + yy
        c = cot[...].reshape(2 * rows, 2 * half_depth)
        grad = dot(c[:, :half_depth], w[0, zz, yy], NT) + dot(c[:, half_depth:], w[1, zz, yy], NT)
        grad = grad.astype(BF16)
        picked = plan[0]
        for image in range(2):
            to = image * heads + head
            grad_rows = grad[image * rows : (image + 1) * rows]
            g_send[to] = grad_rows
            products = grad_rows.astype(F32) * o_two[picked, image, :, columns(head)].astype(F32)
            delta = jnp.sum(products.T, axis=0, keepdims=True)
            lse = lse_two[picked, image, pl.ds(head, 1), :] * math.log2(math.e)
            row = lax.broadcasted_iota(jnp.int32, (8, rows), 0)
            stat_send[to] = jnp.where(row == 0, lse, delta)

            @pl.when(to != me)
            def _():
                remote(g_send.at[to], g.at[me], heads_s.at[3], heads_r.at[3], {"seq": to}).start()
                remote(stat_send.at[to], stat.at[me], heads_s.at[4], heads_r.at[4], {"seq": to}).start()

            @pl.when(to == me)
            def _():
                g[me] = g_send[me]
                stat[me] = stat_send[me]

    def project_group(group):
        at = ring_offset(group)

        @pl.loop(0, group + 1)
        def _(n):
            project(at, ring_offset(n))

        if group > 0:

            @pl.loop(0, group)
            def _(n):
                project(ring_offset(n), at)

    project_group(0)
    start_forward(0)
    for p in range(2):
        first[p][4].wait_recv()
        first[p][5].wait_recv()
        start_second(p, 3)
    for group in range(1, 4):
        start_forward(group)
        if group > 1:
            project_group(group - 1)
        for p in range(2):
            for copy in forward[p, group - 1]:
                copy.wait_recv()
    for p in range(2):
        for copy in forward[p, 3]:
            copy.wait_recv()
    project_group(3)

    channels = pieces.shape[3]

    def piece(to):
        return cot.at[:, :, pl.ds(pl.multiple_of(to * channels, channels), channels)]

    own_piece = local(piece(section), pieces.at[section], own_sem.at[3])
    own_piece.start()

    @pl.loop(1, 4)
    def _(step):
        to = (section + step) % 4
        remote(piece(to), pieces.at[section], piece_s, piece_r, {"section": to}).start()

    for sem, (send, held) in enumerate(((k_send, k), (q_send, q), (v_send, v), (g_send, g), (stat_send, stat))):
        arrived(send, held, sem)

    for source in range(devices):
        lse_row[:, source * rows : (source + 1) * rows] = stat[source, 0:1, :]
        delta_row[:, source * rows : (source + 1) * rows] = stat[source, 1:2, :]

    total = devices * rows
    my_image, my_columns = me // heads, columns(me % heads)

    def give_back(send, out, sem, source):
        place = out.at[my_image, :, my_columns]

        @pl.when(source != me)
        def _():
            remote(send.at[source], place, back_s.at[sem], back_r.at[sem], {"seq": source}).start()

        @pl.when(source == me)
        def _():
            local(send.at[source], place, own_sem.at[sem]).start()

    dq_sum[...] = jnp.zeros_like(dq_sum)
    key_blocks = 8
    query_blocks = 4

    @pl.loop(0, devices // key_blocks)
    def _(u):
        us = pl.ds(u * key_blocks, key_blocks)
        kb = k[us].reshape(key_blocks * rows, head_size)
        vb = v[us].reshape(key_blocks * rows, head_size)
        kt = kb.T

        def inner(t, carry):
            sum_k, sum_v = carry
            qb = q[pl.ds(t * query_blocks, query_blocks)].reshape(query_blocks * rows, head_size)
            gb = g[pl.ds(t * query_blocks, query_blocks)].reshape(query_blocks * rows, head_size)
            ts = pl.ds(pl.multiple_of(t * query_blocks * rows, query_blocks * rows), query_blocks * rows)
            p = jnp.exp2(dot(kb, qb, NT) * scale2 - lse_row[:, ts])
            sum_v = sum_v + dot(p.astype(BF16), gb, NN)
            ds = (p * (dot(vb, gb, NT) - delta_row[:, ts])).astype(BF16)
            sum_k = sum_k + dot(ds, qb, NN)
            dq_sum[:, ts] += dot(kt, ds, NN)
            return sum_k, sum_v

        zeros = jnp.zeros((key_blocks * rows, head_size), F32)
        sum_k, sum_v = lax.fori_loop(0, devices // query_blocks, inner, (zeros, zeros), unroll=4)
        k_send[us] = (sum_k * scale).astype(BF16).reshape(key_blocks, rows, head_size)
        v_send[us] = sum_v.astype(BF16).reshape(key_blocks, rows, head_size)

        @pl.loop(0, key_blocks)
        def _(n):
            give_back(k_send, dk_out, 0, u * key_blocks + n)
            give_back(v_send, dv_out, 1, u * key_blocks + n)

    for source in range(devices):
        q_send[source] = (dq_sum[:, source * rows : (source + 1) * rows] * scale).T.astype(BF16)
        give_back(q_send, dq_out, 2, source)

    own_piece.wait()
    three = pl.ds(0, 3)
    local(pieces.at[three], pieces.at[three], piece_r).wait()
    local(pieces.at[three], pieces.at[three], piece_s).wait()
    for j in range(control_out.shape[0]):
        source, factor = control_map[j], control_scale[j]
        for image in range(2):
            control_out[j, image] = (factor * pieces[source, image].astype(F32)).astype(BF16)

    for copies in list(first.values()) + list(second.values()) + list(forward.values()) + [swaps]:
        for copy in copies:
            copy.wait_send()
    some = pl.ds(0, devices - 1)
    for sem, (send, out) in enumerate(((k_send, dk_out), (v_send, dv_out), (q_send, dq_out))):
        local(send.at[some], send.at[some], back_s.at[sem]).wait()
        local(send.at[some], send.at[some], back_r.at[sem]).wait()
        local(send.at[me], out.at[my_image, :, my_columns], own_sem.at[sem]).wait()


def shards(
    saved_q,
    saved_k,
    saved_v,
    saved_o,
    saved_lse,
    cotangent,
    out_weight,
    plan,
    control_map,
    control_scale,
):
    micro, images, rows, width = saved_q.shape[1:]
    head_count = saved_lse.shape[4]
    head_size = width // head_count
    devices = images * head_count
    depth = cotangent.shape[3]
    sections = lax.axis_size("section")
    channels = depth // sections
    controls = control_map.shape[0]
    rows_out = jax.ShapeDtypeStruct((images, rows, width), BF16)
    two = pltpu.VMEM((micro, images, rows, width), BF16)
    blocks = pltpu.VMEM((devices, rows, head_size), BF16)
    stats = pltpu.VMEM((devices, 8, rows), F32)
    row = pltpu.VMEM((1, devices * rows), F32)
    anywhere = pl.BlockSpec(memory_space=pl.ANY)
    scalars = pl.BlockSpec(memory_space=pltpu.SMEM)
    dma = pltpu.SemaphoreType.DMA
    total = devices * rows
    dq, dk, dv, control = pl.pallas_call(
        kernel,
        out_shape=(
            rows_out,
            rows_out,
            rows_out,
            jax.ShapeDtypeStruct((controls, images, rows, channels), BF16),
        ),
        in_specs=[scalars] * 3 + [anywhere] * 7,
        out_specs=(anywhere, anywhere, anywhere, pl.BlockSpec(memory_space=pltpu.VMEM)),
        scratch_shapes=[two] * 4
        + [
            pltpu.VMEM((micro, images, head_count, rows), F32),
            pltpu.VMEM((images, rows, depth), BF16),
            pltpu.VMEM((2, 4, 4, rows, depth // 2), BF16),
        ]
        + [blocks] * 4
        + [stats]
        + [blocks] * 4
        + [stats, row, row]
        + [
            pltpu.VMEM((head_size, total), F32),
            pltpu.VMEM((sections, images, rows, channels), BF16),
            dma((8,)),
            dma((2,)),
            dma((2,)),
            dma((2, 22)),
            dma((2, 22)),
            dma((5,)),
            dma((5,)),
            dma((3,)),
            dma((3,)),
            dma((4,)),
            dma(()),
            dma(()),
        ],
        compiler_params=pltpu.CompilerParams(
            collective_id=0, has_side_effects=True, vmem_limit_bytes=58 * 2**20
        ),
        cost_estimate=pl.CostEstimate(
            flops=10 * total * total * head_size, bytes_accessed=32 * total * head_size, transcendentals=0
        ),
        name="attention_backward",
    )(
        plan,
        control_map,
        control_scale,
        saved_q[0],
        saved_k[0],
        saved_v[0],
        saved_o[0],
        saved_lse[0].transpose(0, 1, 3, 2),
        cotangent[0],
        out_weight[0],
    )
    return (dq[None], dk[None], dv[None], control)


def solution(mesh):
    placed = (
        P("section", None, None, "seq", None),
        P("section", None, None, "seq", None),
        P("section", None, None, "seq", None),
        P("section", None, None, "seq", None),
        P("section", None, None, "seq", None),
        P("section", None, "seq", None),
        P("section", "seq", None),
        P("section"),
        P(),
        P(),
    )
    return jax.shard_map(
        shards,
        mesh=mesh,
        in_specs=placed,
        out_specs=(
            P("section", None, "seq", None),
            P("section", None, "seq", None),
            P("section", None, "seq", None),
            P(None, None, "seq", "section"),
        ),
        check_vma=False,
    )
```

```python
import functools
import math

import jax
import jax.numpy as jnp
from jax import lax
from jax.experimental import pallas as pl
from jax.experimental.pallas import tpu as pltpu
from jax.sharding import PartitionSpec as P

F32 = jnp.float32
BF16 = jnp.bfloat16
NT = (((1,), (1,)), ((), ()))
NN = (((1,), (0,)), ((), ()))


def dot(a, b, dims):
    return lax.dot_general(a, b, dims, preferred_element_type=F32)


def ring_offset(i):
    return i + (i // 2) * (1 - 2 * (i % 2))


def kernel(
    plan,
    control_map,
    control_scale,
    q_in,
    k_in,
    v_in,
    o_in,
    lse_in,
    cot_in,
    w_in,
    dq_out,
    dk_out,
    dv_out,
    control_out,
    first_two,
    second_two,
    lse_two,
    cot,
    w,
    q_send,
    k_send,
    v_send,
    o_send,
    stat_send,
    q,
    k,
    v,
    o,
    g,
    stat,
    lse_row,
    delta_row,
    kept,
    dq_sum,
    pieces,
    load_sem,
    swap_s,
    swap_r,
    ring_s,
    ring_r,
    heads_s,
    heads_r,
    back_s,
    back_r,
    own_sem,
    piece_s,
    piece_r,
):
    me = lax.axis_index("seq")
    section = lax.axis_index("section")
    z, y, x = me // 8, (me // 2) % 4, me % 2
    devices, rows, head_size = q.shape
    heads = devices // 2
    half_rows, half_depth = w.shape[3:]
    scale = head_size**-0.5
    scale2 = scale * math.log2(math.e)

    def index_of(z, y, x):
        return ((z + 4) % 4) * 8 + ((y + 4) % 4) * 2 + x % 2

    def peer(slot):
        run, dz = slot // 4, slot % 4
        return index_of(z + dz, y + dz + run // 2, x + run + dz)

    def slot_at(to):
        dz, dy, dx = z - to // 8 + 4, y - (to // 2) % 4 + 4, x - to % 2 + 2
        return (((dy - dz + 8) % 4) * 2 + (dx + dz) % 2) * 4 + dz % 4

    def columns(head):
        return pl.ds(pl.multiple_of(head * head_size, head_size), head_size)

    def remote(src, dst, send, recv, device):
        return pltpu.make_async_remote_copy(
            src_ref=src,
            dst_ref=dst,
            send_sem=send,
            recv_sem=recv,
            device_id=device,
            device_id_type=pl.DeviceIdType.MESH,
        )

    def local(src, dst, sem):
        return pltpu.make_async_copy(src, dst, sem)

    loads = [
        local(src, dst, load_sem.at[i])
        for i, (src, dst) in enumerate(
            (
                (k_in, first_two),
                (q_in, second_two),
                (lse_in, lse_two),
                (v_in, first_two),
                (o_in, second_two),
                (cot_in, cot.at[0]),
            )
        )
    ]
    for i in (0, 1, 2, 5):
        loads[i].start()

    def part_columns(part):
        return pl.ds(part * half_depth, half_depth)

    own_w = [local(w_in.at[:, part_columns(p)], w.at[p, z, y], load_sem.at[6 + p]) for p in range(2)]
    for copy in own_w:
        copy.start()
    barrier = pltpu.get_barrier_semaphore()

    @pl.loop(1, devices)
    def _(step):
        pl.semaphore_signal(
            barrier, inc=1, device_id={"seq": peer(step)}, device_id_type=pl.DeviceIdType.MESH
        )

    @pl.loop(1, 4)
    def _(step):
        pl.semaphore_signal(
            barrier, inc=1, device_id={"section": (section + step) % 4}, device_id_type=pl.DeviceIdType.MESH
        )

    pl.semaphore_wait(barrier, devices + 2)

    def turn(part, first, second):
        return (first, second) if part == 0 else (second, first)

    def block(part, first, second):
        dz, dy = turn(part, first, second)
        return w.at[part, (z + dz + 4) % 4, (y + dy + 4) % 4]

    def hop(part, where, to, rows_of, sem, src=None):
        dst = block(part, *where)
        if rows_of is not None:
            dst = dst.at[rows_of]
        dz, dy = turn(part, *to)
        return remote(
            dst if src is None else src,
            dst,
            ring_s.at[part, sem],
            ring_r.at[part, sem],
            {"seq": index_of(z + dz, y + dy, x)},
        )

    low, high = pl.ds(0, half_rows // 2), pl.ds(half_rows // 2, half_rows // 2)
    first, second, forward = {}, {}, {}
    def start_second(p, group):
        at = ring_offset(group)
        src = w_in.at[:, part_columns(p)] if group == 0 else None
        second[p, group] = [
            hop(p, (at, 0), (0, 1), None, 4 + 4 * group, src),
            hop(p, (at, 0), (0, -1), None, 5 + 4 * group, src),
        ]
        for copy in second[p, group]:
            copy.start()

    for p in range(2):
        src = w_in.at[:, part_columns(p)]
        first[p] = [hop(p, (0, 0), (1, 0), None, 0, src), hop(p, (0, 0), (-1, 0), None, 1, src)]
        for copy in first[p]:
            copy.start()
    swap = remote(cot_in, cot.at[1], swap_s, swap_r, {"seq": index_of(z, y, x + 1)})
    swap.start()
    for p in range(2):
        start_second(p, 0)

    def select(two, send, held, sem):
        picked = plan[0]

        @pl.loop(0, 2)
        def _(image):
            for head in range(heads):
                send[image * heads + head] = two[picked, image, :, head * head_size : (head + 1) * head_size]

        held[0] = send[me]

        @pl.loop(1, devices)
        def _(step):
            to = peer(step)
            remote(send.at[to], held.at[slot_at(to)], heads_s.at[sem], heads_r.at[sem], {"seq": to}).start()

    some = pl.ds(0, devices - 1)

    def sent(send, sem):
        local(send.at[some], send.at[some], heads_s.at[sem]).wait()

    def arrived(held, sem):
        local(held.at[some], held.at[some], heads_r.at[sem]).wait()

    loads[0].wait()
    select(first_two, k_send, k, 0)
    loads[1].wait()
    select(second_two, q_send, q, 1)
    loads[2].wait()
    for image in range(2):
        for head in range(heads):
            lse = lse_two[plan[0], image, head : head + 1, :] * math.log2(math.e)
            stat_send[image * heads + head] = jnp.broadcast_to(lse, (8, rows))
    stat[0] = stat_send[me]

    @pl.loop(1, devices)
    def _(step):
        to = peer(step)
        remote(stat_send.at[to], stat.at[slot_at(to)], heads_s.at[5], heads_r.at[5], {"seq": to}).start()

    loads[3].start()
    loads[4].start()
    for copy in own_w:
        copy.wait()
    for p in range(2):
        first[p][0].wait_recv()
        first[p].append(hop(p, (-1, 0), (1, 0), low, 2))
        first[p][2].start()
        first[p][1].wait_recv()
        first[p].append(hop(p, (1, 0), (-1, 0), high, 3))
        first[p][3].start()
    for p in range(2):
        start_second(p, 1)
        start_second(p, 2)
    loads[3].wait()
    select(first_two, v_send, v, 2)

    def start_forward(group):
        at = ring_offset(group)
        for p in range(2):
            second[p, group][0].wait_recv()
            forward[p, group] = [hop(p, (at, -1), (0, 1), low, 6 + 4 * group)]
            forward[p, group][0].start()
            second[p, group][1].wait_recv()
            forward[p, group].append(hop(p, (at, 1), (0, -1), high, 7 + 4 * group))
            forward[p, group][1].start()

    start_forward(0)
    for p in range(2):
        first[p][2].wait_recv()
        first[p][3].wait_recv()
        start_second(p, 3)
    loads[4].wait()
    select(second_two, o_send, o, 3)
    for group in range(1, 4):
        start_forward(group)
    for group in range(4):
        for p in range(2):
            for copy in forward[p, group]:
                copy.wait_recv()
    loads[5].wait()
    swap.wait_recv()

    sent(k_send, 0)
    g_send = k_send

    lane = lax.broadcasted_iota(jnp.int32, (rows, head_size), 1)

    @pl.loop(0, 4)
    def _(zz):
        c = cot[...].reshape(4 * rows, 2 * half_depth)
        w0 = w[0, zz].reshape(4 * half_rows, half_depth)
        w1 = w[1, zz].reshape(4 * half_rows, half_depth)
        grad = dot(c[:, :half_depth], w0, NT) + dot(c[:, half_depth:], w1, NT)
        for image in range(2):
            for pair in range(2):
                cols = slice(pair * head_size, (pair + 1) * head_size)
                mine = grad[image * rows : (image + 1) * rows, cols]
                other = grad[(2 + image) * rows : (3 + image) * rows, cols]
                even = jnp.where(lane < head_size // 2, mine, pltpu.roll(other, head_size // 2, 1))
                odd = jnp.where(lane < head_size // 2, pltpu.roll(mine, head_size // 2, 1), other)
                for n, half in enumerate((even, odd)):
                    to = image * heads + zz * 4 + pair * 2 + n
                    g_send[to] = half.astype(BF16)

                    @pl.when(to != me)
                    def _():
                        remote(
                            g_send.at[to], g.at[slot_at(to)], heads_s.at[4], heads_r.at[4], {"seq": to}
                        ).start()

                    @pl.when(to == me)
                    def _():
                        g[0] = g_send[me]

    channels = pieces.shape[3]

    def piece(to):
        return cot.at[0, :, :, pl.ds(pl.multiple_of(to * channels, channels), channels)]

    own_piece = local(piece(section), pieces.at[section], own_sem.at[3])
    own_piece.start()

    @pl.loop(1, 4)
    def _(step):
        to = (section + step) % 4
        remote(piece(to), pieces.at[section], piece_s, piece_r, {"section": to}).start()

    key_blocks = 4
    query_blocks = 8
    key_rows = key_blocks * rows
    query_rows = query_blocks * rows

    def keys_of(ref, u):
        return ref[pl.ds(u * key_blocks, key_blocks)].reshape(key_rows, head_size)

    def queries_of(ref, t):
        return ref[pl.ds(t * query_blocks, query_blocks)].reshape(query_rows, head_size)

    def row_of(ref, t):
        return ref[:, pl.ds(pl.multiple_of(t * query_rows, query_rows), query_rows)]

    def probabilities(kb, qb, t):
        return jnp.exp2(dot(kb, qb, NT) * scale2 - row_of(lse_row, t))

    arrived(k, 0)
    arrived(q, 1)
    arrived(stat, 5)
    for source in range(devices):
        lse_row[:, source * rows : (source + 1) * rows] = stat[source, 0:1, :]

    @pl.loop(0, kept.shape[0])
    def _(u):
        kb = keys_of(k, u)

        def keep(t, carry):
            kept[u, t] = probabilities(kb, queries_of(q, t), t).astype(BF16)
            return carry

        lax.fori_loop(0, devices // query_blocks, keep, 0, unroll=4)

    arrived(v, 2)
    arrived(o, 3)
    arrived(g, 4)
    for sem, send in ((1, q_send), (2, v_send), (3, o_send), (4, g_send), (5, stat_send)):
        sent(send, sem)

    low_lane = lane < head_size // 2
    for pair in range(devices // 2):
        slots = (pair // 4 * 8 + pair % 4, pair // 4 * 8 + pair % 4 + 4)
        a, b = g[slots[0]].astype(F32), g[slots[1]].astype(F32)
        straight = ((x + pair % 4) % 2) == 0
        one, two = jnp.where(low_lane, a, b), jnp.where(low_lane, b, a)
        one = jnp.where(straight, one, pltpu.roll(one, head_size // 2, 1))
        two = jnp.where(straight, pltpu.roll(two, head_size // 2, 1), two)
        for slot, joined in zip(slots, (one, two)):
            g[slot] = joined.astype(BF16)
            products = joined * o[slot].astype(F32)
            delta_row[:, slot * rows : (slot + 1) * rows] = jnp.sum(products.T, axis=0, keepdims=True)

    total = devices * rows
    my_image, my_columns = me // heads, columns(me % heads)

    def give_back(send, out, sem, slot):
        place = out.at[my_image, :, my_columns]

        @pl.when(slot != 0)
        def _():
            remote(send.at[slot], place, back_s.at[sem], back_r.at[sem], {"seq": peer(slot)}).start()

        @pl.when(slot == 0)
        def _():
            local(send.at[slot], place, own_sem.at[sem]).start()

    dq_sum[...] = jnp.zeros_like(dq_sum)

    def key_block(u, have):
        kb, vb = keys_of(k, u), keys_of(v, u)
        kt = kb.T

        def inner(t, carry):
            sum_k, sum_v = carry
            qb, gb = queries_of(q, t), queries_of(g, t)
            if have:
                rounded = kept[u, t]
                p = rounded.astype(F32)
            else:
                p = probabilities(kb, qb, t)
                rounded = p.astype(BF16)
            sum_v = sum_v + dot(rounded, gb, NN)
            ds = (p * (dot(vb, gb, NT) - row_of(delta_row, t))).astype(BF16)
            sum_k = sum_k + dot(ds, qb, NN)
            dq_sum[:, pl.ds(pl.multiple_of(t * query_rows, query_rows), query_rows)] += dot(kt, ds, NN)
            return sum_k, sum_v

        zeros = jnp.zeros((key_rows, head_size), F32)
        sum_k, sum_v = lax.fori_loop(0, devices // query_blocks, inner, (zeros, zeros), unroll=4)
        slots = pl.ds(u * key_blocks, key_blocks)
        k_send[slots] = (sum_k * scale).astype(BF16).reshape(key_blocks, rows, head_size)
        v_send[slots] = sum_v.astype(BF16).reshape(key_blocks, rows, head_size)

        @pl.loop(0, key_blocks)
        def _(n):
            give_back(k_send, dk_out, 0, u * key_blocks + n)
            give_back(v_send, dv_out, 1, u * key_blocks + n)

    @pl.loop(0, kept.shape[0])
    def _(u):
        key_block(u, True)

    @pl.loop(kept.shape[0], devices // key_blocks)
    def _(u):
        key_block(u, False)

    for source in range(devices):
        q_send[source] = (dq_sum[:, source * rows : (source + 1) * rows] * scale).T.astype(BF16)
        give_back(q_send, dq_out, 2, source)

    own_piece.wait()
    three = pl.ds(0, 3)
    local(pieces.at[three], pieces.at[three], piece_r).wait()
    local(pieces.at[three], pieces.at[three], piece_s).wait()
    for j in range(control_out.shape[0]):
        source, factor = control_map[j], control_scale[j]
        for image in range(2):
            control_out[j, image] = (factor * pieces[source, image].astype(F32)).astype(BF16)

    for copies in list(first.values()) + list(second.values()) + list(forward.values()) + [[swap]]:
        for copy in copies:
            copy.wait_send()
    for sem, (send, out) in enumerate(((k_send, dk_out), (v_send, dv_out), (q_send, dq_out))):
        local(send.at[some], send.at[some], back_s.at[sem]).wait()
        local(send.at[some], send.at[some], back_r.at[sem]).wait()
        local(send.at[0], out.at[my_image, :, my_columns], own_sem.at[sem]).wait()


def shards(
    saved_q,
    saved_k,
    saved_v,
    saved_o,
    saved_lse,
    cotangent,
    out_weight,
    plan,
    control_map,
    control_scale,
):
    micro, images, rows, width = saved_q.shape[1:]
    head_count = saved_lse.shape[4]
    head_size = width // head_count
    devices = images * head_count
    depth = cotangent.shape[3]
    sections = lax.axis_size("section")
    channels = depth // sections
    controls = control_map.shape[0]
    rows_out = jax.ShapeDtypeStruct((images, rows, width), BF16)
    two = pltpu.VMEM((micro, images, rows, width), BF16)
    blocks = pltpu.VMEM((devices, rows, head_size), BF16)
    stats = pltpu.VMEM((devices, 8, rows), F32)
    row = pltpu.VMEM((1, devices * rows), F32)
    anywhere = pl.BlockSpec(memory_space=pl.ANY)
    scalars = pl.BlockSpec(memory_space=pltpu.SMEM)
    dma = pltpu.SemaphoreType.DMA
    total = devices * rows
    dq, dk, dv, control = pl.pallas_call(
        kernel,
        out_shape=(
            rows_out,
            rows_out,
            rows_out,
            jax.ShapeDtypeStruct((controls, images, rows, channels), BF16),
        ),
        in_specs=[scalars] * 3 + [anywhere] * 7,
        out_specs=(anywhere, anywhere, anywhere, pl.BlockSpec(memory_space=pltpu.VMEM)),
        scratch_shapes=[two] * 2
        + [
            pltpu.VMEM((micro, images, head_count, rows), F32),
            pltpu.VMEM((2, images, rows, depth), BF16),
            pltpu.VMEM((2, 4, 4, rows // 2, depth // 2), BF16),
        ]
        + [blocks] * 4
        + [stats]
        + [blocks] * 5
        + [stats, row, row]
        + [
            pltpu.VMEM((6, 4, total // 8, total // 4), BF16),
            pltpu.VMEM((head_size, total), F32),
            pltpu.VMEM((sections, images, rows, channels), BF16),
            dma((8,)),
            dma(()),
            dma(()),
            dma((2, 20)),
            dma((2, 20)),
            dma((6,)),
            dma((6,)),
            dma((3,)),
            dma((3,)),
            dma((4,)),
            dma(()),
            dma(()),
        ],
        compiler_params=pltpu.CompilerParams(
            collective_id=0, has_side_effects=True, vmem_limit_bytes=62 * 2**20
        ),
        cost_estimate=pl.CostEstimate(
            flops=10 * total * total * head_size, bytes_accessed=32 * total * head_size, transcendentals=0
        ),
        name="attention_backward",
    )(
        plan,
        control_map,
        control_scale,
        saved_q[0],
        saved_k[0],
        saved_v[0],
        saved_o[0],
        saved_lse[0].transpose(0, 1, 3, 2),
        cotangent[0],
        out_weight[0],
    )
    return (dq[None], dk[None], dv[None], control)


def solution(mesh):
    placed = (
        P("section", None, None, "seq", None),
        P("section", None, None, "seq", None),
        P("section", None, None, "seq", None),
        P("section", None, None, "seq", None),
        P("section", None, None, "seq", None),
        P("section", None, "seq", None),
        P("section", "seq", None),
        P("section"),
        P(),
        P(),
    )
    return jax.shard_map(
        shards,
        mesh=mesh,
        in_specs=placed,
        out_specs=(
            P("section", None, "seq", None),
            P("section", None, "seq", None),
            P("section", None, "seq", None),
            P(None, None, "seq", "section"),
        ),
        check_vma=False,
    )
```

```python
import functools
import math

import jax
import jax.numpy as jnp
from jax import lax
from jax.experimental import pallas as pl
from jax.experimental.pallas import tpu as pltpu
from jax.sharding import PartitionSpec as P

F32 = jnp.float32
BF16 = jnp.bfloat16
NT = (((1,), (1,)), ((), ()))
NN = (((1,), (0,)), ((), ()))


def dot(a, b, dims):
    return lax.dot_general(a, b, dims, preferred_element_type=F32)


def ring_offset(i):
    return i + (i // 2) * (1 - 2 * (i % 2))


def kernel(
    plan,
    control_map,
    control_scale,
    q_in,
    k_in,
    v_in,
    o_in,
    lse_in,
    cot_in,
    w_in,
    dq_out,
    dk_out,
    dv_out,
    control_out,
    first_two,
    second_two,
    lse_two,
    cot,
    w,
    q_send,
    k_send,
    v_send,
    o_send,
    stat_send,
    q,
    k,
    v,
    o,
    g,
    stat,
    lse_row,
    delta_row,
    kept,
    dq_sum,
    dk_sum,
    pieces,
    load_sem,
    swap_s,
    swap_r,
    ring_s,
    ring_r,
    heads_s,
    heads_r,
    back_s,
    back_r,
    own_sem,
    piece_s,
    piece_r,
):
    me = lax.axis_index("seq")
    section = lax.axis_index("section")
    z, y, x = me // 8, (me // 2) % 4, me % 2
    devices, rows, head_size = q.shape
    heads = devices // 2
    half_rows, half_depth = w.shape[3:]
    scale = head_size**-0.5
    scale2 = scale * math.log2(math.e)

    def index_of(z, y, x):
        return ((z + 4) % 4) * 8 + ((y + 4) % 4) * 2 + x % 2

    def peer(slot):
        run, dz = slot // 4, slot % 4
        return index_of(z + dz, y + dz + run // 2, x + run + dz)

    def slot_at(to):
        dz, dy, dx = z - to // 8 + 4, y - (to // 2) % 4 + 4, x - to % 2 + 2
        return (((dy - dz + 8) % 4) * 2 + (dx + dz) % 2) * 4 + dz % 4

    def columns(head):
        return pl.ds(pl.multiple_of(head * head_size, head_size), head_size)

    def remote(src, dst, send, recv, device):
        return pltpu.make_async_remote_copy(
            src_ref=src,
            dst_ref=dst,
            send_sem=send,
            recv_sem=recv,
            device_id=device,
            device_id_type=pl.DeviceIdType.MESH,
        )

    def local(src, dst, sem):
        return pltpu.make_async_copy(src, dst, sem)

    loads = [
        local(src, dst, load_sem.at[i])
        for i, (src, dst) in enumerate(
            (
                (k_in, first_two),
                (q_in, second_two),
                (lse_in, lse_two),
                (v_in, first_two),
                (o_in, second_two),
                (cot_in, cot.at[0]),
            )
        )
    ]
    for i in (0, 1, 2, 5):
        loads[i].start()

    def part_columns(part):
        return pl.ds(part * half_depth, half_depth)

    own_w = [local(w_in.at[:, part_columns(p)], w.at[p, z, y], load_sem.at[6 + p]) for p in range(2)]
    for copy in own_w:
        copy.start()
    barrier = pltpu.get_barrier_semaphore()

    @pl.loop(1, devices)
    def _(step):
        pl.semaphore_signal(
            barrier, inc=1, device_id={"seq": peer(step)}, device_id_type=pl.DeviceIdType.MESH
        )

    @pl.loop(1, 4)
    def _(step):
        pl.semaphore_signal(
            barrier, inc=1, device_id={"section": (section + step) % 4}, device_id_type=pl.DeviceIdType.MESH
        )

    pl.semaphore_wait(barrier, devices + 2)

    def turn(part, first, second):
        return (first, second) if part == 0 else (second, first)

    def block(part, first, second):
        dz, dy = turn(part, first, second)
        return w.at[part, (z + dz + 4) % 4, (y + dy + 4) % 4]

    def hop(part, where, to, rows_of, sem, src=None):
        dst = block(part, *where)
        if rows_of is not None:
            dst = dst.at[rows_of]
        dz, dy = turn(part, *to)
        return remote(
            dst if src is None else src,
            dst,
            ring_s.at[part, sem],
            ring_r.at[part, sem],
            {"seq": index_of(z + dz, y + dy, x)},
        )

    low, high = pl.ds(0, half_rows // 2), pl.ds(half_rows // 2, half_rows // 2)
    first, second, forward = {}, {}, {}
    def start_second(p, group):
        at = ring_offset(group)
        src = w_in.at[:, part_columns(p)] if group == 0 else None
        second[p, group] = [
            hop(p, (at, 0), (0, 1), None, 4 + 4 * group, src),
            hop(p, (at, 0), (0, -1), None, 5 + 4 * group, src),
        ]
        for copy in second[p, group]:
            copy.start()

    for p in range(2):
        src = w_in.at[:, part_columns(p)]
        first[p] = [hop(p, (0, 0), (1, 0), None, 0, src), hop(p, (0, 0), (-1, 0), None, 1, src)]
        for copy in first[p]:
            copy.start()
    swap = remote(cot_in, cot.at[1], swap_s, swap_r, {"seq": index_of(z, y, x + 1)})
    swap.start()
    for p in range(2):
        start_second(p, 0)

    def select(two, send, held, sem):
        picked = plan[0]

        @pl.loop(0, 2)
        def _(image):
            for head in range(heads):
                send[image * heads + head] = two[picked, image, :, head * head_size : (head + 1) * head_size]

        held[0] = send[me]

        @pl.loop(1, devices)
        def _(step):
            to = peer(step)
            remote(send.at[to], held.at[slot_at(to)], heads_s.at[sem], heads_r.at[sem], {"seq": to}).start()

    some = pl.ds(0, devices - 1)

    def sent(send, sem):
        local(send.at[some], send.at[some], heads_s.at[sem]).wait()

    def arrived(held, sem):
        local(held.at[some], held.at[some], heads_r.at[sem]).wait()

    loads[0].wait()
    select(first_two, k_send, k, 0)
    loads[1].wait()
    select(second_two, q_send, q, 1)
    loads[2].wait()
    for image in range(2):
        for head in range(heads):
            lse = lse_two[plan[0], image, head : head + 1, :] * math.log2(math.e)
            stat_send[image * heads + head] = jnp.broadcast_to(lse, (8, rows))
    stat[0] = stat_send[me]

    @pl.loop(1, devices)
    def _(step):
        to = peer(step)
        remote(stat_send.at[to], stat.at[slot_at(to)], heads_s.at[5], heads_r.at[5], {"seq": to}).start()

    loads[3].start()
    loads[4].start()
    for copy in own_w:
        copy.wait()
    for p in range(2):
        first[p][0].wait_recv()
        first[p].append(hop(p, (-1, 0), (1, 0), low, 2))
        first[p][2].start()
        first[p][1].wait_recv()
        first[p].append(hop(p, (1, 0), (-1, 0), high, 3))
        first[p][3].start()
    for p in range(2):
        start_second(p, 1)
        start_second(p, 2)

    def start_forward(group):
        at = ring_offset(group)
        for p in range(2):
            second[p, group][0].wait_recv()
            forward[p, group] = [hop(p, (at, -1), (0, 1), low, 6 + 4 * group)]
            forward[p, group][0].start()
            second[p, group][1].wait_recv()
            forward[p, group].append(hop(p, (at, 1), (0, -1), high, 7 + 4 * group))
            forward[p, group][1].start()

    start_forward(0)
    for p in range(2):
        first[p][2].wait_recv()
        first[p][3].wait_recv()
        start_second(p, 3)
    for group in range(1, 4):
        start_forward(group)
    for group in range(4):
        for p in range(2):
            for copy in forward[p, group]:
                copy.wait_recv()
    loads[5].wait()
    swap.wait_recv()

    sent(k_send, 0)
    g_send = k_send

    lane = lax.broadcasted_iota(jnp.int32, (rows, head_size), 1)

    @pl.loop(0, 4)
    def _(zz):
        c = cot[...].reshape(4 * rows, 2 * half_depth)
        w0 = w[0, zz].reshape(4 * half_rows, half_depth)
        w1 = w[1, zz].reshape(4 * half_rows, half_depth)
        grad = dot(c[:, :half_depth], w0, NT) + dot(c[:, half_depth:], w1, NT)
        for image in range(2):
            for pair in range(2):
                cols = slice(pair * head_size, (pair + 1) * head_size)
                mine = grad[image * rows : (image + 1) * rows, cols]
                other = grad[(2 + image) * rows : (3 + image) * rows, cols]
                even = jnp.where(lane < head_size // 2, mine, pltpu.roll(other, head_size // 2, 1))
                odd = jnp.where(lane < head_size // 2, pltpu.roll(mine, head_size // 2, 1), other)
                for n, half in enumerate((even, odd)):
                    to = image * heads + zz * 4 + pair * 2 + n
                    g_send[to] = half.astype(BF16)

                    @pl.when(to != me)
                    def _():
                        remote(
                            g_send.at[to], g.at[slot_at(to)], heads_s.at[4], heads_r.at[4], {"seq": to}
                        ).start()

                    @pl.when(to == me)
                    def _():
                        g[0] = g_send[me]

    loads[4].wait()
    select(second_two, o_send, o, 3)

    loads[3].wait()
    select(first_two, v_send, v, 2)

    channels = pieces.shape[3]

    def piece(to):
        return cot.at[0, :, :, pl.ds(pl.multiple_of(to * channels, channels), channels)]

    own_piece = local(piece(section), pieces.at[section], own_sem.at[3])
    own_piece.start()

    @pl.loop(1, 4)
    def _(step):
        to = (section + step) % 4
        remote(piece(to), pieces.at[section], piece_s, piece_r, {"section": to}).start()

    total = devices * rows
    my_image, my_columns = me // heads, columns(me % heads)

    def give_back(send, out, sem, slot):
        place = out.at[my_image, :, my_columns]

        @pl.when(slot != 0)
        def _():
            remote(send.at[slot], place, back_s.at[sem], back_r.at[sem], {"seq": peer(slot)}).start()

        @pl.when(slot == 0)
        def _():
            local(send.at[slot], place, own_sem.at[sem]).start()

    key_blocks = 4
    query_blocks = 8
    key_rows = key_blocks * rows
    query_rows = query_blocks * rows

    def keys_of(ref, u):
        return ref[pl.ds(u * key_blocks, key_blocks)].reshape(key_rows, head_size)

    def queries_of(ref, t):
        return ref[pl.ds(t * query_blocks, query_blocks)].reshape(query_rows, head_size)

    def row_of(ref, t):
        return ref[:, pl.ds(pl.multiple_of(t * query_rows, query_rows), query_rows)]

    def probabilities(kb, qb, t):
        return jnp.exp2(dot(kb, qb, NT) * scale2 - row_of(lse_row, t))

    arrived(k, 0)
    arrived(q, 1)
    arrived(stat, 5)
    for source in range(devices):
        lse_row[:, source * rows : (source + 1) * rows] = stat[source, 0:1, :]

    @pl.loop(0, kept.shape[0])
    def _(u):
        kb = keys_of(k, u)

        def keep(t, carry):
            kept[u, t] = probabilities(kb, queries_of(q, t), t).astype(BF16)
            return carry

        lax.fori_loop(0, devices // query_blocks, keep, 0, unroll=4)

    arrived(g, 4)

    low_lane = lane < head_size // 2
    for pair in range(devices // 2):
        slots = (pair // 4 * 8 + pair % 4, pair // 4 * 8 + pair % 4 + 4)
        a, b = g[slots[0]].astype(F32), g[slots[1]].astype(F32)
        straight = ((x + pair % 4) % 2) == 0
        one, two = jnp.where(low_lane, a, b), jnp.where(low_lane, b, a)
        one = jnp.where(straight, one, pltpu.roll(one, head_size // 2, 1))
        two = jnp.where(straight, pltpu.roll(two, head_size // 2, 1), two)
        for slot, joined in zip(slots, (one, two)):
            g[slot] = joined.astype(BF16)

    sent(q_send, 1)

    def give_values(u, sum_v):
        q_send[pl.ds(u * key_blocks, key_blocks)] = sum_v.astype(BF16).reshape(key_blocks, rows, head_size)

        @pl.loop(0, key_blocks)
        def _(n):
            give_back(q_send, dv_out, 1, u * key_blocks + n)

    @pl.loop(0, kept.shape[0])
    def _(u):
        def inner(t, sum_v):
            return sum_v + dot(kept[u, t], queries_of(g, t), NN)

        zeros = jnp.zeros((key_rows, head_size), F32)
        give_values(u, lax.fori_loop(0, devices // query_blocks, inner, zeros, unroll=4))

    arrived(v, 2)
    arrived(o, 3)
    for sem, send in ((2, v_send), (3, o_send), (4, g_send), (5, stat_send)):
        sent(send, sem)
    for slot in range(devices):
        products = g[slot].astype(F32) * o[slot].astype(F32)
        delta_row[:, slot * rows : (slot + 1) * rows] = jnp.sum(products.T, axis=0, keepdims=True)

    dq_sum[...] = jnp.zeros_like(dq_sum)

    def key_block(u, have):
        kb, vb = keys_of(k, u), keys_of(v, u)
        kt = kb.T

        def inner(t, carry):
            sum_k, sum_v = carry
            qb, gb = queries_of(q, t), queries_of(g, t)
            if have:
                p = kept[u, t].astype(F32)
            else:
                p = probabilities(kb, qb, t)
                sum_v = sum_v + dot(p.astype(BF16), gb, NN)
            ds = (p * (dot(vb, gb, NT) - row_of(delta_row, t))).astype(BF16)
            sum_k = sum_k + dot(ds, qb, NN)
            dq_sum[:, pl.ds(pl.multiple_of(t * query_rows, query_rows), query_rows)] += dot(kt, ds, NN)
            return sum_k, sum_v

        zeros = jnp.zeros((key_rows, head_size), F32)
        sum_k, sum_v = lax.fori_loop(
            0, devices // query_blocks, inner, (zeros, None if have else zeros), unroll=4
        )
        slots = pl.ds(u * key_blocks, key_blocks)
        k_send[slots] = (sum_k * scale).astype(BF16).reshape(key_blocks, rows, head_size)

        @pl.loop(0, key_blocks)
        def _(n):
            give_back(k_send, dk_out, 0, u * key_blocks + n)

        if not have:
            give_values(u, sum_v)

    early = 3

    @pl.loop(kept.shape[0], devices // key_blocks)
    def _(u):
        key_block(u, False)

    @pl.loop(0, early)
    def _(u):
        key_block(u, True)

    late = kept.shape[0] - early
    dk_sum[...] = jnp.zeros_like(dk_sum)

    @pl.loop(0, devices // query_blocks)
    def _(t):
        qb, gb = queries_of(q, t), queries_of(g, t)
        sum_q = dq_sum[:, pl.ds(pl.multiple_of(t * query_rows, query_rows), query_rows)]
        for n in range(late):
            u = early + n
            kb, vb = keys_of(k, u), keys_of(v, u)
            p = kept[u, t].astype(F32)
            ds = (p * (dot(vb, gb, NT) - row_of(delta_row, t))).astype(BF16)
            dk_sum[n * key_rows : (n + 1) * key_rows, :] += dot(ds, qb, NN)
            sum_q = sum_q + dot(kb.T, ds, NN)
        back = (sum_q * scale).T.astype(BF16)
        v_send[pl.ds(t * query_blocks, query_blocks)] = back.reshape(query_blocks, rows, head_size)

        @pl.loop(0, query_blocks)
        def _(n):
            give_back(v_send, dq_out, 2, t * query_blocks + n)

    late_slots = late * key_blocks
    k_send[pl.ds(early * key_blocks, late_slots)] = (
        (dk_sum[...] * scale).astype(BF16).reshape(late_slots, rows, head_size)
    )

    @pl.loop(0, late_slots)
    def _(n):
        give_back(k_send, dk_out, 0, early * key_blocks + n)

    own_piece.wait()
    three = pl.ds(0, 3)
    local(pieces.at[three], pieces.at[three], piece_r).wait()
    local(pieces.at[three], pieces.at[three], piece_s).wait()
    for j in range(control_out.shape[0]):
        source, factor = control_map[j], control_scale[j]
        for image in range(2):
            control_out[j, image] = (factor * pieces[source, image].astype(F32)).astype(BF16)

    for copies in list(first.values()) + list(second.values()) + list(forward.values()) + [[swap]]:
        for copy in copies:
            copy.wait_send()
    for sem, (send, out) in enumerate(((k_send, dk_out), (q_send, dv_out), (v_send, dq_out))):
        local(send.at[some], send.at[some], back_s.at[sem]).wait()
        local(send.at[some], send.at[some], back_r.at[sem]).wait()
        local(send.at[0], out.at[my_image, :, my_columns], own_sem.at[sem]).wait()


def shards(
    saved_q,
    saved_k,
    saved_v,
    saved_o,
    saved_lse,
    cotangent,
    out_weight,
    plan,
    control_map,
    control_scale,
):
    micro, images, rows, width = saved_q.shape[1:]
    head_count = saved_lse.shape[4]
    head_size = width // head_count
    devices = images * head_count
    depth = cotangent.shape[3]
    sections = lax.axis_size("section")
    channels = depth // sections
    controls = control_map.shape[0]
    rows_out = jax.ShapeDtypeStruct((images, rows, width), BF16)
    two = pltpu.VMEM((micro, images, rows, width), BF16)
    blocks = pltpu.VMEM((devices, rows, head_size), BF16)
    stats = pltpu.VMEM((devices, 8, rows), F32)
    row = pltpu.VMEM((1, devices * rows), F32)
    anywhere = pl.BlockSpec(memory_space=pl.ANY)
    scalars = pl.BlockSpec(memory_space=pltpu.SMEM)
    dma = pltpu.SemaphoreType.DMA
    total = devices * rows
    dq, dk, dv, control = pl.pallas_call(
        kernel,
        out_shape=(
            rows_out,
            rows_out,
            rows_out,
            jax.ShapeDtypeStruct((controls, images, rows, channels), BF16),
        ),
        in_specs=[scalars] * 3 + [anywhere] * 7,
        out_specs=(anywhere, anywhere, anywhere, pl.BlockSpec(memory_space=pltpu.VMEM)),
        scratch_shapes=[two] * 2
        + [
            pltpu.VMEM((micro, images, head_count, rows), F32),
            pltpu.VMEM((2, images, rows, depth), BF16),
            pltpu.VMEM((2, 4, 4, rows // 2, depth // 2), BF16),
        ]
        + [blocks] * 4
        + [stats]
        + [blocks] * 5
        + [stats, row, row]
        + [
            pltpu.VMEM((6, 4, total // 8, total // 4), BF16),
            pltpu.VMEM((head_size, total), F32),
            pltpu.VMEM((total * 3 // 8, head_size), F32),
            pltpu.VMEM((sections, images, rows, channels), BF16),
            dma((8,)),
            dma(()),
            dma(()),
            dma((2, 20)),
            dma((2, 20)),
            dma((6,)),
            dma((6,)),
            dma((3,)),
            dma((3,)),
            dma((4,)),
            dma(()),
            dma(()),
        ],
        compiler_params=pltpu.CompilerParams(
            collective_id=0, has_side_effects=True, vmem_limit_bytes=62 * 2**20
        ),
        cost_estimate=pl.CostEstimate(
            flops=10 * total * total * head_size, bytes_accessed=32 * total * head_size, transcendentals=0
        ),
        name="attention_backward",
    )(
        plan,
        control_map,
        control_scale,
        saved_q[0],
        saved_k[0],
        saved_v[0],
        saved_o[0],
        saved_lse[0].transpose(0, 1, 3, 2),
        cotangent[0],
        out_weight[0],
    )
    return (dq[None], dk[None], dv[None], control)


def solution(mesh):
    placed = (
        P("section", None, None, "seq", None),
        P("section", None, None, "seq", None),
        P("section", None, None, "seq", None),
        P("section", None, None, "seq", None),
        P("section", None, None, "seq", None),
        P("section", None, "seq", None),
        P("section", "seq", None),
        P("section"),
        P(),
        P(),
    )
    return jax.shard_map(
        shards,
        mesh=mesh,
        in_specs=placed,
        out_specs=(
            P("section", None, "seq", None),
            P("section", None, "seq", None),
            P("section", None, "seq", None),
            P(None, None, "seq", "section"),
        ),
        check_vma=False,
    )
```

```python
import functools
import math

import jax
import jax.numpy as jnp
from jax import lax
from jax.experimental import pallas as pl
from jax.experimental.pallas import tpu as pltpu
from jax.sharding import PartitionSpec as P

F32 = jnp.float32
BF16 = jnp.bfloat16
NT = (((1,), (1,)), ((), ()))
NN = (((1,), (0,)), ((), ()))


def dot(a, b, dims):
    return lax.dot_general(a, b, dims, preferred_element_type=F32)


def ring_offset(i):
    return i + (i // 2) * (1 - 2 * (i % 2))


def kernel(
    plan,
    control_map,
    control_scale,
    q_in,
    k_in,
    v_in,
    o_in,
    lse_in,
    cot_in,
    w_in,
    dq_out,
    dk_out,
    dv_out,
    control_out,
    first_two,
    second_two,
    lse_two,
    cot,
    w,
    q_send,
    k_send,
    v_send,
    o_send,
    stat_send,
    q,
    k,
    v,
    o,
    g,
    stat,
    lse_row,
    delta_row,
    kept,
    dq_sum,
    dk_sum,
    pieces,
    load_sem,
    swap_s,
    swap_r,
    ring_s,
    ring_r,
    heads_s,
    heads_r,
    back_s,
    back_r,
    own_sem,
    piece_s,
    piece_r,
):
    me = lax.axis_index("seq")
    section = lax.axis_index("section")
    z, y, x = me // 8, (me // 2) % 4, me % 2
    devices, rows, head_size = q.shape
    heads = devices // 2
    half_rows, half_depth = w.shape[3:]
    scale = head_size**-0.5
    scale2 = scale * math.log2(math.e)

    def index_of(z, y, x):
        return ((z + 4) % 4) * 8 + ((y + 4) % 4) * 2 + x % 2

    def peer(slot):
        run, dz = slot // 4, slot % 4
        return index_of(z + dz, y + dz + run // 2, x + run + dz)

    def slot_at(to):
        dz, dy, dx = z - to // 8 + 4, y - (to // 2) % 4 + 4, x - to % 2 + 2
        return (((dy - dz + 8) % 4) * 2 + (dx + dz) % 2) * 4 + dz % 4

    def columns(head):
        return pl.ds(pl.multiple_of(head * head_size, head_size), head_size)

    def remote(src, dst, send, recv, device):
        return pltpu.make_async_remote_copy(
            src_ref=src,
            dst_ref=dst,
            send_sem=send,
            recv_sem=recv,
            device_id=device,
            device_id_type=pl.DeviceIdType.MESH,
        )

    def local(src, dst, sem):
        return pltpu.make_async_copy(src, dst, sem)

    loads = [
        local(src, dst, load_sem.at[i])
        for i, (src, dst) in enumerate(
            (
                (k_in, first_two),
                (q_in, second_two),
                (lse_in, lse_two),
                (v_in, first_two),
                (o_in, second_two),
                (cot_in, cot.at[0]),
            )
        )
    ]
    for i in (0, 1, 2, 5):
        loads[i].start()

    def part_columns(part):
        return pl.ds(part * half_depth, half_depth)

    own_w = [local(w_in.at[:, part_columns(p)], w.at[p, z, y], load_sem.at[6 + p]) for p in range(2)]
    for copy in own_w:
        copy.start()
    barrier = pltpu.get_barrier_semaphore()

    @pl.loop(1, devices)
    def _(step):
        pl.semaphore_signal(
            barrier, inc=1, device_id={"seq": peer(step)}, device_id_type=pl.DeviceIdType.MESH
        )

    @pl.loop(1, 4)
    def _(step):
        pl.semaphore_signal(
            barrier, inc=1, device_id={"section": (section + step) % 4}, device_id_type=pl.DeviceIdType.MESH
        )

    pl.semaphore_wait(barrier, devices + 2)

    def turn(part, first, second):
        return (first, second) if part == 0 else (second, first)

    def block(part, first, second):
        dz, dy = turn(part, first, second)
        return w.at[part, (z + dz + 4) % 4, (y + dy + 4) % 4]

    def hop(part, where, to, rows_of, sem, src=None):
        dst = block(part, *where)
        if rows_of is not None:
            dst = dst.at[rows_of]
        dz, dy = turn(part, *to)
        return remote(
            dst if src is None else src,
            dst,
            ring_s.at[part, sem],
            ring_r.at[part, sem],
            {"seq": index_of(z + dz, y + dy, x)},
        )

    low, high = pl.ds(0, half_rows // 2), pl.ds(half_rows // 2, half_rows // 2)
    first, second, forward = {}, {}, {}
    def start_second(p, group):
        at = ring_offset(group)
        src = w_in.at[:, part_columns(p)] if group == 0 else None
        second[p, group] = [
            hop(p, (at, 0), (0, 1), None, 4 + 4 * group, src),
            hop(p, (at, 0), (0, -1), None, 5 + 4 * group, src),
        ]
        for copy in second[p, group]:
            copy.start()

    swap = remote(cot_in, cot.at[1], swap_s, swap_r, {"seq": index_of(z, y, x + 1)})
    swap.start()
    for p in range(2):
        src = w_in.at[:, part_columns(p)]
        first[p] = [hop(p, (0, 0), (1, 0), None, 0, src), hop(p, (0, 0), (-1, 0), None, 1, src)]
        for copy in first[p]:
            copy.start()
    for p in range(2):
        start_second(p, 0)

    def select(two, send, held, sem):
        picked = plan[0]

        @pl.loop(0, 2)
        def _(image):
            for head in range(heads):
                send[image * heads + head] = two[picked, image, :, head * head_size : (head + 1) * head_size]

        held[0] = send[me]

        @pl.loop(1, devices)
        def _(step):
            to = peer(step)
            remote(send.at[to], held.at[slot_at(to)], heads_s.at[sem], heads_r.at[sem], {"seq": to}).start()

    some = pl.ds(0, devices - 1)

    def sent(send, sem):
        local(send.at[some], send.at[some], heads_s.at[sem]).wait()

    def arrived(held, sem):
        local(held.at[some], held.at[some], heads_r.at[sem]).wait()

    loads[0].wait()
    select(first_two, k_send, k, 0)
    loads[1].wait()
    select(second_two, q_send, q, 1)
    loads[2].wait()
    for image in range(2):
        for head in range(heads):
            lse = lse_two[plan[0], image, head : head + 1, :] * math.log2(math.e)
            stat_send[image * heads + head] = jnp.broadcast_to(lse, (8, rows))
    stat[0] = stat_send[me]

    @pl.loop(1, devices)
    def _(step):
        to = peer(step)
        remote(stat_send.at[to], stat.at[slot_at(to)], heads_s.at[5], heads_r.at[5], {"seq": to}).start()

    loads[3].start()
    loads[4].start()
    for copy in own_w:
        copy.wait()
    for p in range(2):
        first[p][0].wait_recv()
        first[p].append(hop(p, (-1, 0), (1, 0), low, 2))
        first[p][2].start()
        first[p][1].wait_recv()
        first[p].append(hop(p, (1, 0), (-1, 0), high, 3))
        first[p][3].start()
    for p in range(2):
        start_second(p, 1)
        start_second(p, 2)

    def start_forward(group):
        at = ring_offset(group)
        for p in range(2):
            second[p, group][0].wait_recv()
            forward[p, group] = [hop(p, (at, -1), (0, 1), low, 6 + 4 * group)]
            forward[p, group][0].start()
            second[p, group][1].wait_recv()
            forward[p, group].append(hop(p, (at, 1), (0, -1), high, 7 + 4 * group))
            forward[p, group][1].start()

    start_forward(0)
    for p in range(2):
        first[p][2].wait_recv()
        first[p][3].wait_recv()
        start_second(p, 3)
    for group in range(1, 4):
        start_forward(group)
    for group in range(4):
        for p in range(2):
            for copy in forward[p, group]:
                copy.wait_recv()
    loads[5].wait()
    swap.wait_recv()

    sent(k_send, 0)
    g_send = k_send

    lane = lax.broadcasted_iota(jnp.int32, (rows, head_size), 1)

    @pl.loop(0, 4)
    def _(zz):
        c = cot[...].reshape(4 * rows, 2 * half_depth)
        w0 = w[0, zz].reshape(4 * half_rows, half_depth)
        w1 = w[1, zz].reshape(4 * half_rows, half_depth)
        grad = dot(c[:, :half_depth], w0, NT) + dot(c[:, half_depth:], w1, NT)
        for image in range(2):
            for pair in range(2):
                cols = slice(pair * head_size, (pair + 1) * head_size)
                mine = grad[image * rows : (image + 1) * rows, cols]
                other = grad[(2 + image) * rows : (3 + image) * rows, cols]
                even = jnp.where(lane < head_size // 2, mine, pltpu.roll(other, head_size // 2, 1))
                odd = jnp.where(lane < head_size // 2, pltpu.roll(mine, head_size // 2, 1), other)
                for n, half in enumerate((even, odd)):
                    to = image * heads + zz * 4 + pair * 2 + n
                    g_send[to] = half.astype(BF16)

                    @pl.when(to != me)
                    def _():
                        remote(
                            g_send.at[to], g.at[slot_at(to)], heads_s.at[4], heads_r.at[4], {"seq": to}
                        ).start()

                    @pl.when(to == me)
                    def _():
                        g[0] = g_send[me]

    loads[4].wait()
    select(second_two, o_send, o, 3)

    loads[3].wait()
    select(first_two, v_send, v, 2)

    channels = pieces.shape[3]

    def piece(to):
        return cot.at[0, :, :, pl.ds(pl.multiple_of(to * channels, channels), channels)]

    own_piece = local(piece(section), pieces.at[section], own_sem.at[3])
    own_piece.start()

    @pl.loop(1, 4)
    def _(step):
        to = (section + step) % 4
        remote(piece(to), pieces.at[section], piece_s, piece_r, {"section": to}).start()

    total = devices * rows
    my_image, my_columns = me // heads, columns(me % heads)

    def give_back(send, out, sem, slot):
        place = out.at[my_image, :, my_columns]

        @pl.when(slot != 0)
        def _():
            remote(send.at[slot], place, back_s.at[sem], back_r.at[sem], {"seq": peer(slot)}).start()

        @pl.when(slot == 0)
        def _():
            local(send.at[slot], place, own_sem.at[sem]).start()

    key_blocks = 4
    query_blocks = 8
    key_rows = key_blocks * rows
    query_rows = query_blocks * rows

    def keys_of(ref, u):
        return ref[pl.ds(u * key_blocks, key_blocks)].reshape(key_rows, head_size)

    def queries_of(ref, t):
        return ref[pl.ds(t * query_blocks, query_blocks)].reshape(query_rows, head_size)

    def row_of(ref, t):
        return ref[:, pl.ds(pl.multiple_of(t * query_rows, query_rows), query_rows)]

    def probabilities(kb, qb, t):
        return jnp.exp2(dot(kb, qb, NT) * scale2 - row_of(lse_row, t))

    arrived(k, 0)
    arrived(q, 1)
    arrived(stat, 5)
    for source in range(devices):
        lse_row[:, source * rows : (source + 1) * rows] = stat[source, 0:1, :]

    @pl.loop(0, kept.shape[0])
    def _(u):
        kb = keys_of(k, u)

        def keep(t, carry):
            kept[u, t] = probabilities(kb, queries_of(q, t), t).astype(BF16)
            return carry

        lax.fori_loop(0, devices // query_blocks, keep, 0, unroll=4)

    arrived(g, 4)

    low_lane = lane < head_size // 2
    for pair in range(devices // 2):
        slots = (pair // 4 * 8 + pair % 4, pair // 4 * 8 + pair % 4 + 4)
        a, b = g[slots[0]].astype(F32), g[slots[1]].astype(F32)
        straight = ((x + pair % 4) % 2) == 0
        one, two = jnp.where(low_lane, a, b), jnp.where(low_lane, b, a)
        one = jnp.where(straight, one, pltpu.roll(one, head_size // 2, 1))
        two = jnp.where(straight, pltpu.roll(two, head_size // 2, 1), two)
        for slot, joined in zip(slots, (one, two)):
            g[slot] = joined.astype(BF16)

    sent(q_send, 1)

    def give_values(u, sum_v):
        q_send[pl.ds(u * key_blocks, key_blocks)] = sum_v.astype(BF16).reshape(key_blocks, rows, head_size)

        @pl.loop(0, key_blocks)
        def _(n):
            give_back(q_send, dv_out, 1, u * key_blocks + n)

    @pl.loop(0, kept.shape[0])
    def _(u):
        def inner(t, sum_v):
            return sum_v + dot(kept[u, t], queries_of(g, t), NN)

        zeros = jnp.zeros((key_rows, head_size), F32)
        give_values(u, lax.fori_loop(0, devices // query_blocks, inner, zeros, unroll=4))

    arrived(v, 2)
    arrived(o, 3)
    for sem, send in ((2, v_send), (3, o_send), (4, g_send), (5, stat_send)):
        sent(send, sem)
    for slot in range(devices):
        products = g[slot].astype(F32) * o[slot].astype(F32)
        delta_row[:, slot * rows : (slot + 1) * rows] = jnp.sum(products.T, axis=0, keepdims=True)

    dq_sum[...] = jnp.zeros_like(dq_sum)

    def key_block(u, have):
        kb, vb = keys_of(k, u), keys_of(v, u)
        kt = kb.T

        def inner(t, carry):
            sum_k, sum_v = carry
            qb, gb = queries_of(q, t), queries_of(g, t)
            if have:
                p = kept[u, t].astype(F32)
            else:
                p = probabilities(kb, qb, t)
                sum_v = sum_v + dot(p.astype(BF16), gb, NN)
            ds = (p * (dot(vb, gb, NT) - row_of(delta_row, t))).astype(BF16)
            sum_k = sum_k + dot(ds, qb, NN)
            dq_sum[:, pl.ds(pl.multiple_of(t * query_rows, query_rows), query_rows)] += dot(kt, ds, NN)
            return sum_k, sum_v

        zeros = jnp.zeros((key_rows, head_size), F32)
        sum_k, sum_v = lax.fori_loop(
            0, devices // query_blocks, inner, (zeros, None if have else zeros), unroll=4
        )
        slots = pl.ds(u * key_blocks, key_blocks)
        k_send[slots] = (sum_k * scale).astype(BF16).reshape(key_blocks, rows, head_size)

        @pl.loop(0, key_blocks)
        def _(n):
            give_back(k_send, dk_out, 0, u * key_blocks + n)

        if not have:
            give_values(u, sum_v)

    early = 3

    @pl.loop(kept.shape[0], devices // key_blocks)
    def _(u):
        key_block(u, False)

    @pl.loop(0, early)
    def _(u):
        key_block(u, True)

    late = kept.shape[0] - early
    dk_sum[...] = jnp.zeros_like(dk_sum)

    @pl.loop(0, devices // query_blocks)
    def _(t):
        qb, gb = queries_of(q, t), queries_of(g, t)
        sum_q = dq_sum[:, pl.ds(pl.multiple_of(t * query_rows, query_rows), query_rows)]
        for n in range(late):
            u = early + n
            kb, vb = keys_of(k, u), keys_of(v, u)
            p = kept[u, t].astype(F32)
            ds = (p * (dot(vb, gb, NT) - row_of(delta_row, t))).astype(BF16)
            dk_sum[n * key_rows : (n + 1) * key_rows, :] += dot(ds, qb, NN)
            sum_q = sum_q + dot(kb.T, ds, NN)
        back = (sum_q * scale).T.astype(BF16)
        v_send[pl.ds(t * query_blocks, query_blocks)] = back.reshape(query_blocks, rows, head_size)

        @pl.loop(0, query_blocks)
        def _(n):
            give_back(v_send, dq_out, 2, t * query_blocks + n)

    late_slots = late * key_blocks
    k_send[pl.ds(early * key_blocks, late_slots)] = (
        (dk_sum[...] * scale).astype(BF16).reshape(late_slots, rows, head_size)
    )

    @pl.loop(0, late_slots)
    def _(n):
        give_back(k_send, dk_out, 0, early * key_blocks + n)

    own_piece.wait()
    three = pl.ds(0, 3)
    local(pieces.at[three], pieces.at[three], piece_r).wait()
    local(pieces.at[three], pieces.at[three], piece_s).wait()
    for j in range(control_out.shape[0]):
        source, factor = control_map[j], control_scale[j]
        for image in range(2):
            control_out[j, image] = (factor * pieces[source, image].astype(F32)).astype(BF16)

    for copies in list(first.values()) + list(second.values()) + list(forward.values()) + [[swap]]:
        for copy in copies:
            copy.wait_send()
    for sem, (send, out) in enumerate(((k_send, dk_out), (q_send, dv_out), (v_send, dq_out))):
        local(send.at[some], send.at[some], back_s.at[sem]).wait()
        local(send.at[some], send.at[some], back_r.at[sem]).wait()
        local(send.at[0], out.at[my_image, :, my_columns], own_sem.at[sem]).wait()


def shards(
    saved_q,
    saved_k,
    saved_v,
    saved_o,
    saved_lse,
    cotangent,
    out_weight,
    plan,
    control_map,
    control_scale,
):
    micro, images, rows, width = saved_q.shape[1:]
    head_count = saved_lse.shape[4]
    head_size = width // head_count
    devices = images * head_count
    depth = cotangent.shape[3]
    sections = lax.axis_size("section")
    channels = depth // sections
    controls = control_map.shape[0]
    rows_out = jax.ShapeDtypeStruct((images, rows, width), BF16)
    two = pltpu.VMEM((micro, images, rows, width), BF16)
    blocks = pltpu.VMEM((devices, rows, head_size), BF16)
    stats = pltpu.VMEM((devices, 8, rows), F32)
    row = pltpu.VMEM((1, devices * rows), F32)
    anywhere = pl.BlockSpec(memory_space=pl.ANY)
    scalars = pl.BlockSpec(memory_space=pltpu.SMEM)
    dma = pltpu.SemaphoreType.DMA
    total = devices * rows
    dq, dk, dv, control = pl.pallas_call(
        kernel,
        out_shape=(
            rows_out,
            rows_out,
            rows_out,
            jax.ShapeDtypeStruct((controls, images, rows, channels), BF16),
        ),
        in_specs=[scalars] * 3 + [anywhere] * 7,
        out_specs=(anywhere, anywhere, anywhere, pl.BlockSpec(memory_space=pltpu.VMEM)),
        scratch_shapes=[two] * 2
        + [
            pltpu.VMEM((micro, images, head_count, rows), F32),
            pltpu.VMEM((2, images, rows, depth), BF16),
            pltpu.VMEM((2, 4, 4, rows // 2, depth // 2), BF16),
        ]
        + [blocks] * 4
        + [stats]
        + [blocks] * 5
        + [stats, row, row]
        + [
            pltpu.VMEM((6, 4, total // 8, total // 4), BF16),
            pltpu.VMEM((head_size, total), F32),
            pltpu.VMEM((total * 3 // 8, head_size), F32),
            pltpu.VMEM((sections, images, rows, channels), BF16),
            dma((8,)),
            dma(()),
            dma(()),
            dma((2, 20)),
            dma((2, 20)),
            dma((6,)),
            dma((6,)),
            dma((3,)),
            dma((3,)),
            dma((4,)),
            dma(()),
            dma(()),
        ],
        compiler_params=pltpu.CompilerParams(
            collective_id=0, has_side_effects=True, vmem_limit_bytes=62 * 2**20
        ),
        cost_estimate=pl.CostEstimate(
            flops=10 * total * total * head_size, bytes_accessed=32 * total * head_size, transcendentals=0
        ),
        name="attention_backward",
    )(
        plan,
        control_map,
        control_scale,
        saved_q[0],
        saved_k[0],
        saved_v[0],
        saved_o[0],
        saved_lse[0].transpose(0, 1, 3, 2),
        cotangent[0],
        out_weight[0],
    )
    return (dq[None], dk[None], dv[None], control)


def solution(mesh):
    placed = (
        P("section", None, None, "seq", None),
        P("section", None, None, "seq", None),
        P("section", None, None, "seq", None),
        P("section", None, None, "seq", None),
        P("section", None, None, "seq", None),
        P("section", None, "seq", None),
        P("section", "seq", None),
        P("section"),
        P(),
        P(),
    )
    return jax.shard_map(
        shards,
        mesh=mesh,
        in_specs=placed,
        out_specs=(
            P("section", None, "seq", None),
            P("section", None, "seq", None),
            P("section", None, "seq", None),
            P(None, None, "seq", "section"),
        ),
        check_vma=False,
    )
```
